128 devices in a mesh: band: 8 (over x_lo, y), grid: 16 (over z, x_hi, core).
Axes of the slice: x: 4 (x_hi: 2, x_lo: 2; x = x_hi * 2 + x_lo), y: 4, z: 4, core: 2. Of those that a mesh axis runs over, the one named last changes fastest.
Arguments:
- orbitals: float32 [8, 96, 9216], P('band', 'grid'), may hold values from -6.5 to 6.5
- blocks: float32 [128, 96, 9216], P('band', 'grid'), may hold values from -6.5 to 6.5
- owner: int32 [2], replicated, may hold values from 0 to 7, as said below
Outputs:
- local_exchange: float32 [8, 96, 9216], P('band', 'grid')
- block_exchange: float32 [2, 16, 96, 9216], P(None, 'band', 'grid')
The draws below stay inside these ranges and needn't reach their ends.
Inputs may be any that keep to these rules, and one draw needn't show every extreme that they name: `owner`: the 2 rounds name different owners, and one of them is the last index of band.
All inputs are finite; a program needn't handle non-finite values.
Results may differ from the reference program's by a relative error of at most 0.0001.
Values sent between devices are 32-bit elements; how exact they have to be, the bound alone decides.
No kernel may reach another device: no remote copies, remote signals or barrier semaphores. Data moves between devices by JAX's collectives and lax.ppermute only.
A program may use at most 192 MiB of HBM per device.

```python
import math
import jax
import jax.numpy as jnp
from jax import lax

NX = 96
NY = 96
NZ = 96
BLOCK = 16
ROUNDS = 2
NORB = 8
BLOCKS_ALL = 128
N_BAND = 8


def textured(key, rows):
    first = jax.random.fold_in(key, 0)
    shape = (rows, NX, NY * NZ)
    normal = jnp.clip(jax.random.normal(first, shape, jnp.float32), -6.0, 6.0)
    return normal


def draw_orbitals(key, part):
    key = jax.random.fold_in(key, 17)
    return textured(key, NORB)


def draw_blocks(key, part):
    key = jax.random.fold_in(key, 29)
    return textured(key, BLOCKS_ALL)


def draw_owner(key, part):
    key = jax.random.fold_in(key, 41)
    first, second = jax.random.split(key)
    others = jax.random.permutation(first, jnp.arange(N_BAND - 1, dtype=jnp.int32))
    picked = jnp.concatenate([others[:ROUNDS - 1], jnp.full((1,), N_BAND - 1, jnp.int32)])
    placing = jax.random.permutation(second, jnp.arange(ROUNDS, dtype=jnp.int32))
    return picked[placing].astype(jnp.int32)


def setup_inputs(seed: int = 0) -> dict:
    streams_of = jax.random.split(jax.random.key(seed), 4)
    orbitals = draw_orbitals(jax.random.fold_in(streams_of[3], 71), 0)
    blocks = draw_blocks(jax.random.fold_in(streams_of[3], 71), 0)
    owner = draw_owner(jax.random.fold_in(streams_of[3], 71), 0)
    return {"orbitals": orbitals, "blocks": blocks, "owner": owner}


mixing = 0.25
cell_length = 41.04


def signed(length):
    points = jnp.arange(length, dtype=jnp.int32)
    return jnp.where(points < length // 2, points, points - length).astype(jnp.float32)


def coulomb_grid():
    spacing = 2.0 * math.pi / cell_length
    wave_x = signed(NX) * spacing
    wave_y = signed(NY) * spacing
    wave_z = signed(NZ) * spacing
    squared = wave_x[:, None, None] * wave_x[:, None, None] + wave_y[None, :, None] * wave_y[None, :, None] + wave_z[None, None, :] * wave_z[None, None, :]
    safe = jnp.where(squared > 0, squared, jnp.float32(1.0))
    return jnp.where(squared > 0, 4.0 * math.pi / safe, jnp.float32(0.0)).astype(jnp.float32)


def potential(pair_field, kernel):
    spectrum = jnp.fft.fftn(pair_field, axes=(1, 2, 3))
    return jnp.real(jnp.fft.ifftn(spectrum * kernel, axes=(1, 2, 3))).astype(jnp.float32)


def reference(orbitals, blocks, owner):
    fields = orbitals.reshape(NORB, NX, NY, NZ)
    stacks = blocks.reshape(N_BAND, BLOCK, NX, NY, NZ)
    kernel = coulomb_grid()
    running = jnp.zeros((NORB, NX, NY, NZ), jnp.float32)
    collected = []
    for turn_index in range(ROUNDS):
        chosen = lax.dynamic_index_in_dim(stacks, owner[turn_index].astype(jnp.int32), 0, keepdims=False)

        def visit(carry, block_row):
            values = potential(block_row[None] * fields, kernel)
            return carry + block_row[None] * values, jnp.sum(fields * values, axis=0)

        running, block_terms = lax.scan(visit, running, chosen)
        collected.append(block_terms)
    local_exchange = (-mixing * running).reshape(NORB, NX, NY * NZ)
    block_exchange = (-mixing * jnp.stack(collected)).reshape(ROUNDS, BLOCK, NX, NY * NZ)
    return local_exchange, block_exchange
```

```python
import math

import jax
import jax.numpy as jnp
import ml_dtypes
import numpy as np
from jax import lax
from jax.experimental import pallas as pl
from jax.experimental.pallas import tpu as pltpu
from jax.sharding import Mesh, PartitionSpec as P

N = 96
LANES = 128
FOLD = 4
ROWS = N // FOLD
WIDTH = FOLD * N
ROUNDS = 2
mixing = 0.25
cell_length = 41.04
SCALE = -mixing * 4.0 * math.pi / ((2.0 * math.pi / cell_length) ** 2 * N**3)
f32 = jnp.float32
bf16 = jnp.bfloat16


def trig(rows, columns):
    angle = 2.0 * np.pi * ((rows[:, None] * columns[None, :]) % N) / N
    return np.cos(angle), np.sin(angle)


def two_parts(table):
    high = table.astype(ml_dtypes.bfloat16)
    low = (table - high.astype(np.float64)).astype(ml_dtypes.bfloat16)
    return high, low


def right_table(sign):
    points = np.arange(N)
    cosine, sine = trig(points, points)
    table = np.zeros((2 * LANES, 2 * LANES))
    table[:N, :N] = cosine
    table[:N, LANES : LANES + N] = sign * sine
    table[LANES : LANES + N, :N] = -sign * sine
    table[LANES : LANES + N, LANES : LANES + N] = cosine
    return two_parts(table)


def left_table(sign, out_points, in_points):
    cosine, sine = trig(out_points, in_points)
    table = np.block([[cosine, -sign * sine], [sign * sine, cosine]])
    high, low = two_parts(table)
    return np.concatenate([high, low], axis=0), high


natural = np.arange(N)
folded = (np.arange(N) % ROWS) * FOLD + np.arange(N) // ROWS
Z_FWD = right_table(-1.0)
Z_INV = right_table(1.0)
Y_FWD = left_table(-1.0, natural, folded)
Y_INV = left_table(1.0, folded, natural)
SUB = 6
PLANES = 4 * SUB
X_FWD = left_table(-1.0, natural, natural)
X_INV = left_table(1.0, natural, natural)


def split(value):
    high = value.astype(bf16)
    return high, (value - high.astype(f32)).astype(bf16)


def dot(a, b):
    return jnp.dot(a, b, preferred_element_type=f32)


def times_right(value, high_ref, low_ref):
    high, low = split(value)
    return dot(high, high_ref[...]) + dot(low, high_ref[...]) + dot(high, low_ref[...])


def times_left(both_ref, high_ref, value):
    high, low = split(value)
    first = dot(both_ref[...], high)
    return first[: 2 * N] + first[2 * N :] + dot(high_ref[...], low)


def unfold(plane):
    lane = lax.broadcasted_iota(jnp.int32, (ROWS, LANES), 1)
    a, b, c = plane[:, :128], plane[:, 128:256], plane[:, 256:]
    return jnp.concatenate(
        [
            a,
            pltpu.roll(jnp.where(lane >= 96, a, b), 32, 1),
            pltpu.roll(jnp.where(lane >= 64, b, c), 64, 1),
            pltpu.roll(c, 96, 1),
        ],
        axis=0,
    )


def fold(field):
    lane = lax.broadcasted_iota(jnp.int32, (ROWS, LANES), 1)
    parts = [field[i * ROWS : (i + 1) * ROWS] for i in range(FOLD)]
    second = pltpu.roll(parts[1], 96, 1)
    third = pltpu.roll(parts[2], 64, 1)
    return jnp.concatenate(
        [
            jnp.where(lane < 96, parts[0], second),
            jnp.where(lane < 64, second, third),
            jnp.where(lane < 32, third, pltpu.roll(parts[3], 32, 1)),
        ],
        axis=1,
    )


def pick(core, own, other):
    first = jnp.where(core == 0, own, other)
    second = jnp.where(core == 0, other, own)
    return first, second


def forward_kernel(ids, phi_ref, own, other, zh, zl, yb, yh, re_ref, im_ref):
    core = ids[0]
    for half in range(2):
        for p in range(SUB):
            reals = pick(core, own[0, 0, half, p], other[0, 0, half, p])
            imags = pick(core, own[0, 1, half, p], other[0, 1, half, p])
            rows = []
            for c in range(2):
                phi = phi_ref[0, 2 * half + c, p]
                rows.append(
                    jnp.concatenate([unfold(phi * reals[c]), unfold(phi * imags[c])], axis=1)
                )
            lines = times_right(jnp.concatenate(rows, axis=0), zh, zl)
            first, second = lines[:N], lines[N:]
            field = jnp.concatenate(
                [
                    jnp.concatenate([first[:, :LANES], second[:, :LANES]], axis=1),
                    jnp.concatenate([first[:, LANES:], second[:, LANES:]], axis=1),
                ],
                axis=0,
            )
            spectrum = times_left(yb, yh, field)
            for c in range(2):
                at = pl.ds((half * 2 + c) * SUB + p, N, stride=PLANES)
                lanes = slice(c * LANES, (c + 1) * LANES)
                re_ref[at, :] = spectrum[:N, lanes]
                im_ref[at, :] = spectrum[N:, lanes]


def middle_kernel(re_in, im_in, fb, fh, ib, ih, re_out, im_out):
    step = pl.program_id(0)
    rows = re_in.shape[1]
    x = lax.broadcasted_iota(jnp.int32, (N, 2 * LANES), 0)
    lane = lax.broadcasted_iota(jnp.int32, (N, 2 * LANES), 1)
    z = lane % LANES

    def wave(i):
        return jnp.where(i < N // 2, i, i - N)

    plane = wave(x) ** 2 + wave(z) ** 2
    for pair in range(rows // 2):
        value = jnp.concatenate(
            [
                jnp.concatenate([part[k, 2 * pair], part[k, 2 * pair + 1]], axis=1)
                for part in (re_in, im_in)
                for k in range(4)
            ],
            axis=0,
        )
        y = step * rows + 2 * pair + lane // LANES
        square = plane + wave(y) ** 2
        weight = jnp.where(square > 0, SCALE / jnp.maximum(square, 1).astype(f32), 0.0)
        spectrum = times_left(fb, fh, value)
        spectrum = jnp.concatenate([spectrum[:N] * weight, spectrum[N:] * weight], axis=0)
        value = times_left(ib, ih, spectrum)
        for i, part in enumerate((re_out, im_out)):
            for k in range(4):
                at = (4 * i + k) * PLANES
                for j in range(2):
                    part[k, 2 * pair + j] = value[
                        at : at + PLANES, j * LANES : (j + 1) * LANES
                    ]


def inverse_kernel(
    ids, phi_ref, own, other, re_ref, im_ref, yb, yh, zh, zl, keep, send, local_ref
):
    core = ids[0]
    for half in range(2):
        for p in range(SUB):
            loaded = []
            for c in range(2):
                at = pl.ds((half * 2 + c) * SUB + p, N, stride=PLANES)
                loaded.append((re_ref[at, :], im_ref[at, :]))
            value = jnp.concatenate(
                [
                    jnp.concatenate([loaded[0][0], loaded[1][0]], axis=1),
                    jnp.concatenate([loaded[0][1], loaded[1][1]], axis=1),
                ],
                axis=0,
            )
            value = times_left(yb, yh, value)
            lines = jnp.concatenate(
                [
                    jnp.concatenate([value[:N, :LANES], value[N:, :LANES]], axis=1),
                    jnp.concatenate([value[:N, LANES:], value[N:, LANES:]], axis=1),
                ],
                axis=0,
            )
            lines = times_right(lines, zh, zl)
            reals = pick(core, own[0, 0, half, p], other[0, 0, half, p])
            imags = pick(core, own[0, 1, half, p], other[0, 1, half, p])
            terms = []
            for c in range(2):
                real = fold(lines[c * N : (c + 1) * N, :LANES])
                imag = fold(lines[c * N : (c + 1) * N, LANES:])
                at = 2 * half + c
                phi = phi_ref[0, at, p]
                local_ref[at, 0, p] = reals[c] * real + imags[c] * imag
                terms.append((phi * real, phi * imag))
            for r in range(2):
                keep[0, r, half, p] = jnp.where(core == 0, terms[0][r], terms[1][r])
                send[0, r, half, p] = jnp.where(core == 0, terms[1][r], terms[0][r])


def whole(table):
    return pl.BlockSpec(table.shape, lambda *_: (0,) * table.ndim)


PARAMS = pltpu.CompilerParams(vmem_limit_bytes=56 * 2**20)
FLOPS = 2 * 3 * N * N * 4 * N * N * 2


PIECE = (2, 2, SUB, ROWS, WIDTH)


def piece_spec():
    return pl.BlockSpec((1, *PIECE), lambda i, ids: (i, 0, 0, 0, 0, 0))


def phi_spec():
    return pl.BlockSpec((1, 4, SUB, ROWS, WIDTH), lambda i, ids: ((ids[1] + i) & 3, 0, 0, 0, 0))


def spectrum_spec():
    return pl.BlockSpec((N * PLANES, LANES), lambda i, ids: (i, 0))


def forward_planes(ids, phi, own, other):
    tables = [jnp.asarray(t) for t in (*Z_FWD, *Y_FWD)]
    return pl.pallas_call(
        forward_kernel,
        grid_spec=pltpu.PrefetchScalarGridSpec(
            num_scalar_prefetch=1,
            grid=(4,),
            in_specs=[phi_spec(), piece_spec(), piece_spec()] + [whole(t) for t in tables],
            out_specs=[spectrum_spec()] * 2,
        ),
        out_shape=[jax.ShapeDtypeStruct((4 * N * PLANES, LANES), f32)] * 2,
        compiler_params=PARAMS,
        cost_estimate=pl.CostEstimate(
            flops=2 * FLOPS, bytes_accessed=20_000_000, transcendentals=0
        ),
    )(ids, phi, own, other, *tables)


def middle_lines(real, imag):
    per = 8
    tables = [jnp.asarray(t) for t in (*X_FWD, *X_INV)]
    shape = (4, N, PLANES, LANES)
    spec = pl.BlockSpec((4, per, PLANES, LANES), lambda i: (0, i, 0, 0))
    out = pl.pallas_call(
        middle_kernel,
        grid=(N // per,),
        in_specs=[spec] * 2 + [whole(t) for t in tables],
        out_specs=[spec] * 2,
        out_shape=[jax.ShapeDtypeStruct(shape, f32)] * 2,
        compiler_params=PARAMS,
        cost_estimate=pl.CostEstimate(
            flops=2 * FLOPS, bytes_accessed=20_000_000, transcendentals=0
        ),
    )(real.reshape(shape), imag.reshape(shape), *tables)
    return [part.reshape(4 * N * PLANES, LANES) for part in out]


def inverse_planes(ids, phi, own, other, real, imag):
    tables = [jnp.asarray(t) for t in (*Y_INV, *Z_INV)]
    return pl.pallas_call(
        inverse_kernel,
        grid_spec=pltpu.PrefetchScalarGridSpec(
            num_scalar_prefetch=1,
            grid=(4,),
            in_specs=[phi_spec(), piece_spec(), piece_spec()]
            + [spectrum_spec()] * 2
            + [whole(t) for t in tables],
            out_specs=[
                piece_spec(),
                piece_spec(),
                pl.BlockSpec((4, 1, SUB, ROWS, WIDTH), lambda i, ids: (0, i, 0, 0, 0)),
            ],
        ),
        out_shape=[jax.ShapeDtypeStruct((4, *PIECE), f32)] * 2
        + [jax.ShapeDtypeStruct((4, 4, SUB, ROWS, WIDTH), f32)],
        compiler_params=PARAMS,
        cost_estimate=pl.CostEstimate(
            flops=2 * FLOPS, bytes_accessed=30_000_000, transcendentals=0
        ),
    )(ids, phi, own, other, real, imag, *tables)


TURN_AXES = ("x_lo", "y", "z", "core")


def turn(value):
    pairs = []
    for a in range(2):
        for y in range(4):
            for z in range(4):
                for c in range(2):
                    source = ((a * 4 + y) * 4 + z) * 2 + c
                    target = ((c * 4 + z) * 4 + y) * 2 + a
                    pairs.append((source, target))
    return lax.ppermute(value, TURN_AXES, pairs)


def other_core(value):
    return lax.ppermute(value, "core", [(0, 1), (1, 0)])


LINE_X = ("x_lo", "x_hi")
RING = {"y": (0, 1, 2, 3), "z": (0, 1, 2, 3), LINE_X: (0, 2, 1, 3)}


def shifted(value, axis, step):
    ring = RING[axis]
    return lax.ppermute(value, axis, [(ring[i], ring[(i + step) % 4]) for i in range(4)])


def ahead(value, axis):
    return shifted(value, axis, 1)


def behind(value, axis):
    return shifted(value, axis, 3)


def halves_of(value):
    size = value.shape[0] // 2
    return value[:size], value[size:]


def gather_ring(mine, axis):
    before = ahead(mine, axis)
    after = behind(mine, axis)
    far = ahead(halves_of(before)[0], axis), behind(halves_of(after)[1], axis)
    return jnp.stack([mine, after, jnp.concatenate(far, axis=0), before])


def scatter_ring(parts, axis):
    first, second = halves_of(parts[2])
    first, second = ahead(first, axis), behind(second, axis)
    after, before = halves_of(parts[1]), halves_of(parts[3])
    after = jnp.concatenate([after[0] + first, after[1]], axis=0)
    before = jnp.concatenate([before[0], before[1] + second], axis=0)
    return parts[0] + ahead(after, axis) + behind(before, axis)


def per_device(orbitals, blocks, owner):
    core = lax.axis_index("core")
    y, z = lax.axis_index("y"), lax.axis_index("z")
    place = 2 * lax.axis_index("x_hi") + lax.axis_index("x_lo")
    ids = jnp.stack([core, z]).astype(jnp.int32)
    planes = orbitals.shape[1]

    phi = turn(orbitals.reshape(planes, ROWS, WIDTH))
    blocks = blocks.reshape(16, planes, ROWS, WIDTH)
    phi, blocks = lax.optimization_barrier((phi, blocks))
    phi = lax.all_gather(phi, ("y", "x_hi", "x_lo")).reshape(4, 4, planes, ROWS, WIDTH)

    blocks = lax.all_to_all(blocks, ("x_lo", "y", "x_hi"), 0, 0, tiled=True)
    blocks = blocks.reshape(8, 2, planes, ROWS, WIDTH)
    mine = jnp.stack(
        [lax.dynamic_index_in_dim(blocks, owner[r], 0, False) for r in range(ROUNDS)]
    )
    own = gather_ring(mine, "z")
    other = other_core(own)

    spectrum = forward_planes(ids, phi, own, other)
    spectrum = middle_lines(*spectrum)
    keep, send, local = inverse_planes(ids, phi, own, other, *spectrum)

    total = keep + other_core(send)
    total = [lax.dynamic_index_in_dim(total, (k - z) & 3, 0, False) for k in range(4)]
    total = lax.psum_scatter(jnp.stack(total), "z", scatter_dimension=0)
    total = lax.all_to_all(total, "x_hi", 1, 1, tiled=True)

    local = [lax.dynamic_index_in_dim(local, (k + place) & 3, 0, False) for k in range(4)]
    local = scatter_ring(local, LINE_X)
    local = [lax.dynamic_index_in_dim(local, (k + y - z) & 3, 0, False) for k in range(4)]
    local = turn(scatter_ring(local, "y"))
    return (
        local.reshape(1, planes, N * N),
        total.reshape(ROUNDS, 2, planes, N * N),
    )


def solution(mesh):
    fine = Mesh(mesh.devices.reshape(2, 4, 4, 2, 2), ("x_lo", "y", "z", "x_hi", "core"))
    band = ("x_lo", "y")
    grid = ("z", "x_hi", "core")
    return jax.shard_map(
        per_device,
        mesh=fine,
        in_specs=(P(band, grid, None), P(band, grid, None), P()),
        out_specs=(P(band, grid, None), P(None, band, grid, None)),
        check_vma=False,
    )
```

```python
import math

import jax
import jax.numpy as jnp
import ml_dtypes
import numpy as np
from jax import lax
from jax.experimental import pallas as pl
from jax.experimental.pallas import tpu as pltpu
from jax.sharding import Mesh, PartitionSpec as P

N = 96
LANES = 128
FOLD = 4
ROWS = N // FOLD
WIDTH = FOLD * N
ROUNDS = 2
mixing = 0.25
cell_length = 41.04
SCALE = -mixing * 4.0 * math.pi / ((2.0 * math.pi / cell_length) ** 2 * N**3)
f32 = jnp.float32
bf16 = jnp.bfloat16


def trig(rows, columns):
    angle = 2.0 * np.pi * ((rows[:, None] * columns[None, :]) % N) / N
    return np.cos(angle), np.sin(angle)


def two_parts(table):
    high = table.astype(ml_dtypes.bfloat16)
    low = (table - high.astype(np.float64)).astype(ml_dtypes.bfloat16)
    return np.concatenate([high, low], axis=0)


def right_table(sign):
    points = np.arange(N)
    cosine, sine = trig(points, points)
    table = np.zeros((2 * LANES, 2 * LANES))
    table[:N, :N] = cosine
    table[:N, LANES : LANES + N] = sign * sine
    table[LANES : LANES + N, :N] = -sign * sine
    table[LANES : LANES + N, LANES : LANES + N] = cosine
    return two_parts(table)


def left_table(sign, out_points, in_points):
    cosine, sine = trig(out_points, in_points)
    return two_parts(np.block([[cosine, -sign * sine], [sign * sine, cosine]]))


natural = np.arange(N)
folded = (np.arange(N) % ROWS) * FOLD + np.arange(N) // ROWS
RIGHT = np.stack([right_table(-1.0), right_table(1.0)])
Z_FWD, Z_INV = 0, 1
LEFT = np.stack(
    [
        left_table(-1.0, natural, folded),
        left_table(1.0, folded, natural),
        left_table(-1.0, natural, natural),
        left_table(1.0, natural, natural),
    ]
)
Y_FWD, Y_INV, X_FWD, X_INV = 0, 1, 2, 3
SUB = 6
PLANES = 4 * SUB


def split(value):
    high = value.astype(bf16)
    return high, (value - high.astype(f32)).astype(bf16)


def dot(a, b):
    return jnp.dot(a, b, preferred_element_type=f32)


def times_right(value, table):
    high, low = split(value)
    above, below = table[: 2 * LANES, :], table[2 * LANES :, :]
    return dot(high, above) + dot(low, above) + dot(high, below)


def times_left(table, value):
    high, low = split(value)
    first = dot(table[...], high)
    return first[: 2 * N] + first[2 * N :] + dot(table[: 2 * N, :], low)


def unfold(plane):
    lane = lax.broadcasted_iota(jnp.int32, (ROWS, LANES), 1)
    a, b, c = plane[:, :128], plane[:, 128:256], plane[:, 256:]
    return jnp.concatenate(
        [
            a,
            pltpu.roll(jnp.where(lane >= 96, a, b), 32, 1),
            pltpu.roll(jnp.where(lane >= 64, b, c), 64, 1),
            pltpu.roll(c, 96, 1),
        ],
        axis=0,
    )


def fold(field):
    lane = lax.broadcasted_iota(jnp.int32, (ROWS, LANES), 1)
    parts = [field[i * ROWS : (i + 1) * ROWS] for i in range(FOLD)]
    second = pltpu.roll(parts[1], 96, 1)
    third = pltpu.roll(parts[2], 64, 1)
    return jnp.concatenate(
        [
            jnp.where(lane < 96, parts[0], second),
            jnp.where(lane < 64, second, third),
            jnp.where(lane < 32, third, pltpu.roll(parts[3], 32, 1)),
        ],
        axis=1,
    )


def pick(core, own, other):
    first = jnp.where(core == 0, own, other)
    second = jnp.where(core == 0, other, own)
    return first, second


FORWARD = 8
MIDDLE = 12
INVERSE = 8
LINES = N // MIDDLE
HELD = N * PLANES


def field_kernel(
    ids, phi_ref, own, other, right, left,
    keep, send, local_ref, re_ref, im_ref
):
    core = ids[0]
    step = pl.program_id(0)

    def forward(near, half):
        base = near * HELD + half * 2 * SUB
        for p in range(SUB):
            reals = pick(core, own[0, 0, 0, p], other[0, 0, 0, p])
            imags = pick(core, own[0, 1, 0, p], other[0, 1, 0, p])
            rows = []
            for c in range(2):
                phi = phi_ref[0, 2 * half + c, p]
                rows.append(
                    jnp.concatenate([unfold(phi * reals[c]), unfold(phi * imags[c])], axis=1)
                )
            lines = times_right(jnp.concatenate(rows, axis=0), right.at[Z_FWD])
            first, second = lines[:N], lines[N:]
            field = jnp.concatenate(
                [
                    jnp.concatenate([first[:, :LANES], second[:, :LANES]], axis=1),
                    jnp.concatenate([first[:, LANES:], second[:, LANES:]], axis=1),
                ],
                axis=0,
            )
            spectrum = times_left(left.at[Y_FWD], field)
            for c in range(2):
                at = pl.ds(base + c * SUB + p, N, stride=PLANES)
                lanes = slice(c * LANES, (c + 1) * LANES)
                re_ref[at, :] = spectrum[:N, lanes]
                im_ref[at, :] = spectrum[N:, lanes]

    def middle(block):
        x = lax.broadcasted_iota(jnp.int32, (N, 2 * LANES), 0)
        lane = lax.broadcasted_iota(jnp.int32, (N, 2 * LANES), 1)

        def wave(i):
            return jnp.where(i < N // 2, i, i - N)

        plane = wave(x) ** 2 + wave(lane % LANES) ** 2

        def at(k, ky):
            return pl.ds(pl.multiple_of(k * HELD + ky * PLANES, 8), PLANES)

        for pair in range(LINES // 2):
            ky = block * LINES + 2 * pair
            value = jnp.concatenate(
                [
                    jnp.concatenate([part[at(k, ky), :], part[at(k, ky + 1), :]], axis=1)
                    for part in (re_ref, im_ref)
                    for k in range(4)
                ],
                axis=0,
            )
            square = plane + wave(ky + lane // LANES) ** 2
            weight = jnp.where(square > 0, SCALE / jnp.maximum(square, 1).astype(f32), 0.0)
            spectrum = times_left(left.at[X_FWD], value)
            spectrum = jnp.concatenate([spectrum[:N] * weight, spectrum[N:] * weight], axis=0)
            value = times_left(left.at[X_INV], spectrum)
            for i, part in enumerate((re_ref, im_ref)):
                for k in range(4):
                    first = (4 * i + k) * PLANES
                    for j in range(2):
                        part[at(k, ky + j), :] = value[
                            first : first + PLANES, j * LANES : (j + 1) * LANES
                        ]

    def inverse(near, half):
        base = near * HELD + half * 2 * SUB
        for p in range(SUB):
            loaded = []
            for c in range(2):
                at = pl.ds(base + c * SUB + p, N, stride=PLANES)
                loaded.append((re_ref[at, :], im_ref[at, :]))
            value = jnp.concatenate(
                [
                    jnp.concatenate([loaded[0][0], loaded[1][0]], axis=1),
                    jnp.concatenate([loaded[0][1], loaded[1][1]], axis=1),
                ],
                axis=0,
            )
            value = times_left(left.at[Y_INV], value)
            lines = jnp.concatenate(
                [
                    jnp.concatenate([value[:N, :LANES], value[N:, :LANES]], axis=1),
                    jnp.concatenate([value[:N, LANES:], value[N:, LANES:]], axis=1),
                ],
                axis=0,
            )
            lines = times_right(lines, right.at[Z_INV])
            reals = pick(core, own[0, 0, 0, p], other[0, 0, 0, p])
            imags = pick(core, own[0, 1, 0, p], other[0, 1, 0, p])
            terms = []
            for c in range(2):
                real = fold(lines[c * N : (c + 1) * N, :LANES])
                imag = fold(lines[c * N : (c + 1) * N, LANES:])
                at = 2 * half + c
                phi = phi_ref[0, at, p]
                local_ref[at, 0, p] = reals[c] * real + imags[c] * imag
                terms.append((phi * real, phi * imag))
            for r in range(2):
                keep[0, r, 0, p] = jnp.where(core == 0, terms[0][r], terms[1][r])
                send[0, r, 0, p] = jnp.where(core == 0, terms[1][r], terms[0][r])

    @pl.when(step < FORWARD)
    def _():
        forward(step // 2, step % 2)

    @pl.when((step >= FORWARD) & (step < FORWARD + MIDDLE))
    def _():
        middle(step - FORWARD)

    @pl.when(step >= FORWARD + MIDDLE)
    def _():
        last = step - (FORWARD + MIDDLE)
        inverse(last // 2, last % 2)


def whole(table):
    return pl.BlockSpec(table.shape, lambda *_: (0,) * table.ndim)


def in_place(step):
    last = step - (FORWARD + MIDDLE)
    at = jnp.where(step < FORWARD, step, jnp.maximum(last, 0))
    return at // 2, at % 2


def out_place(step):
    at = jnp.maximum(step - (FORWARD + MIDDLE), 0)
    return at // 2, at % 2


PIECE = (2, 2, SUB, ROWS, WIDTH)


def solve(ids, phi, own, other):
    tables = [jnp.asarray(RIGHT), jnp.asarray(LEFT)]
    block = (1, 2, 1, SUB, ROWS, WIDTH)

    def phi_at(step, ids):
        return ((ids[1] + in_place(step)[0]) & 3, 0, 0, 0, 0)

    def block_at(step, ids):
        near, half = in_place(step)
        return (near, 0, half, 0, 0, 0)

    def term_at(step, ids):
        near, half = out_place(step)
        return (near, 0, half, 0, 0, 0)

    def local_at(step, ids):
        return (0, (ids[2] + out_place(step)[0]) & 3, 0, 0, 0)

    return pl.pallas_call(
        field_kernel,
        grid_spec=pltpu.PrefetchScalarGridSpec(
            num_scalar_prefetch=1,
            grid=(FORWARD + MIDDLE + INVERSE,),
            in_specs=[
                pl.BlockSpec((1, 4, SUB, ROWS, WIDTH), phi_at),
                pl.BlockSpec(block, block_at),
                pl.BlockSpec(block, block_at),
            ]
            + [whole(t) for t in tables],
            out_specs=[
                pl.BlockSpec(block, term_at),
                pl.BlockSpec(block, term_at),
                pl.BlockSpec((4, 1, SUB, ROWS, WIDTH), local_at),
            ],
            scratch_shapes=[pltpu.VMEM((4 * HELD, LANES), f32)] * 2,
        ),
        out_shape=[jax.ShapeDtypeStruct((4, *PIECE), f32)] * 2
        + [jax.ShapeDtypeStruct((4, 4, SUB, ROWS, WIDTH), f32)],
        compiler_params=pltpu.CompilerParams(vmem_limit_bytes=48 * 2**20),
        cost_estimate=pl.CostEstimate(
            flops=2 * 3 * 6 * (2 * N) ** 2 * N * N, bytes_accessed=35_000_000, transcendentals=0
        ),
    )(ids, phi, own, other, *tables)


TURN_AXES = ("x_lo", "y", "z", "core")


def turn(value):
    pairs = []
    for a in range(2):
        for y in range(4):
            for z in range(4):
                for c in range(2):
                    source = ((a * 4 + y) * 4 + z) * 2 + c
                    target = ((c * 4 + z) * 4 + y) * 2 + a
                    pairs.append((source, target))
    return lax.ppermute(value, TURN_AXES, pairs)


def other_core(value):
    return lax.ppermute(value, "core", [(0, 1), (1, 0)])


LINE_X = ("x_lo", "x_hi")
RING = {"y": (0, 1, 2, 3), "z": (0, 1, 2, 3), LINE_X: (0, 2, 1, 3)}


def shifted(value, axis, step):
    ring = RING[axis]
    return lax.ppermute(value, axis, [(ring[i], ring[(i + step) % 4]) for i in range(4)])


def ahead(value, axis):
    return shifted(value, axis, 1)


def behind(value, axis):
    return shifted(value, axis, 3)


def halves_of(value):
    size = (value.shape[0] + 1) // 2
    return value[:size], value[size:]


def gather_ring(mine, axis):
    before = ahead(mine, axis)
    after = behind(mine, axis)
    far = ahead(halves_of(before)[0], axis), behind(halves_of(after)[1], axis)
    return jnp.stack([mine, after, jnp.concatenate(far, axis=0), before])


def scatter_ring(parts, axis):
    first, second = halves_of(parts[2])
    first, second = ahead(first, axis), behind(second, axis)
    after, before = halves_of(parts[1]), halves_of(parts[3])
    after = jnp.concatenate([after[0] + first, after[1]], axis=0)
    before = jnp.concatenate([before[0], before[1] + second], axis=0)
    return parts[0] + ahead(after, axis) + behind(before, axis)


def per_device(orbitals, blocks, owner):
    core, y, z = (lax.axis_index(name) for name in ("core", "y", "z"))
    ids = jnp.stack([core, z, (z - y) & 3]).astype(jnp.int32)
    planes = orbitals.shape[1]

    phi = turn(orbitals.reshape(planes, ROWS, WIDTH))
    blocks = blocks.reshape(16, planes, ROWS, WIDTH)
    phi, blocks = lax.optimization_barrier((phi, blocks))
    phi = lax.all_gather(phi, ("y", "x_hi", "x_lo")).reshape(4, 4, planes, ROWS, WIDTH)

    blocks = lax.all_to_all(blocks, ("x_lo", "y", "x_hi"), 0, 0, tiled=True)
    blocks = blocks.reshape(8, 2, planes, ROWS, WIDTH)
    mine = jnp.stack(
        [lax.dynamic_index_in_dim(blocks, owner[r], 0, False) for r in range(ROUNDS)]
    )
    own = gather_ring(mine, "z")
    other = other_core(own)

    keep, send, local = solve(ids, phi, own, other)

    local = lax.psum_scatter(local, ("x_hi", "x_lo"), scatter_dimension=0)
    total = scatter_ring(keep + other_core(send), "z")
    total, local = lax.optimization_barrier((total, local))
    local = scatter_ring(local, "y")
    total = lax.all_to_all(total, "x_hi", 1, 1, tiled=True)
    local = turn(local)
    return (
        local.reshape(1, planes, N * N),
        total.reshape(ROUNDS, 2, planes, N * N),
    )


def solution(mesh):
    fine = Mesh(mesh.devices.reshape(2, 4, 4, 2, 2), ("x_lo", "y", "z", "x_hi", "core"))
    band = ("x_lo", "y")
    grid = ("z", "x_hi", "core")
    return jax.shard_map(
        per_device,
        mesh=fine,
        in_specs=(P(band, grid, None), P(band, grid, None), P()),
        out_specs=(P(band, grid, None), P(None, band, grid, None)),
        check_vma=False,
    )
```

```python
import math

import jax
import jax.numpy as jnp
import ml_dtypes
import numpy as np
from jax import lax
from jax.experimental import pallas as pl
from jax.experimental.pallas import tpu as pltpu
from jax.sharding import Mesh, PartitionSpec as P

N = 96
LANES = 128
FOLD = 4
ROWS = N // FOLD
WIDTH = FOLD * N
ROUNDS = 2
mixing = 0.25
cell_length = 41.04
SCALE = -mixing * 4.0 * math.pi / ((2.0 * math.pi / cell_length) ** 2 * N**3)
f32 = jnp.float32
bf16 = jnp.bfloat16


def trig(rows, columns):
    angle = 2.0 * np.pi * ((rows[:, None] * columns[None, :]) % N) / N
    return np.cos(angle), np.sin(angle)


def two_parts(table):
    high = table.astype(ml_dtypes.bfloat16)
    low = (table - high.astype(np.float64)).astype(ml_dtypes.bfloat16)
    return np.concatenate([high, low], axis=0)


def right_table(sign):
    points = np.arange(N)
    cosine, sine = trig(points, points)
    table = np.zeros((2 * LANES, 2 * LANES))
    table[:N, :N] = cosine
    table[:N, LANES : LANES + N] = sign * sine
    table[LANES : LANES + N, :N] = -sign * sine
    table[LANES : LANES + N, LANES : LANES + N] = cosine
    return two_parts(table)


def left_table(sign, out_points, in_points):
    cosine, sine = trig(out_points, in_points)
    return two_parts(np.block([[cosine, -sign * sine], [sign * sine, cosine]]))


natural = np.arange(N)
folded = (np.arange(N) % ROWS) * FOLD + np.arange(N) // ROWS
RIGHT = np.stack([right_table(-1.0), right_table(1.0)])
Z_FWD, Z_INV = 0, 1
LEFT = np.stack(
    [
        left_table(-1.0, natural, folded),
        left_table(1.0, folded, natural),
        left_table(-1.0, natural, natural),
        left_table(1.0, natural, natural),
    ]
)
Y_FWD, Y_INV, X_FWD, X_INV = 0, 1, 2, 3
SUB = 6
PLANES = 4 * SUB


def split(value):
    high = value.astype(bf16)
    return high, (value - high.astype(f32)).astype(bf16)


def dot(a, b):
    return jnp.dot(a, b, preferred_element_type=f32)


def times_right(value, table):
    high, low = split(value)
    above, below = table[: 2 * LANES, :], table[2 * LANES :, :]
    return dot(high, above) + dot(low, above) + dot(high, below)


def times_left(table, value):
    high, low = split(value)
    first = dot(table[...], high)
    return first[: 2 * N] + first[2 * N :] + dot(table[: 2 * N, :], low)


def unfold(plane):
    lane = lax.broadcasted_iota(jnp.int32, (ROWS, LANES), 1)
    a, b, c = plane[:, :128], plane[:, 128:256], plane[:, 256:]
    return jnp.concatenate(
        [
            a,
            pltpu.roll(jnp.where(lane >= 96, a, b), 32, 1),
            pltpu.roll(jnp.where(lane >= 64, b, c), 64, 1),
            pltpu.roll(c, 96, 1),
        ],
        axis=0,
    )


def fold(field):
    lane = lax.broadcasted_iota(jnp.int32, (ROWS, LANES), 1)
    parts = [field[i * ROWS : (i + 1) * ROWS] for i in range(FOLD)]
    second = pltpu.roll(parts[1], 96, 1)
    third = pltpu.roll(parts[2], 64, 1)
    return jnp.concatenate(
        [
            jnp.where(lane < 96, parts[0], second),
            jnp.where(lane < 64, second, third),
            jnp.where(lane < 32, third, pltpu.roll(parts[3], 32, 1)),
        ],
        axis=1,
    )


def pick(core, own, other):
    first = jnp.where(core == 0, own, other)
    second = jnp.where(core == 0, other, own)
    return first, second


FORWARD = 4
MIDDLE = 3
INVERSE = 4
LINES = N // MIDDLE
HELD = N * PLANES


def field_kernel(
    ids, phi_ref, own, other, right, left,
    keep, send, local_ref, re_ref, im_ref
):
    core = ids[0]
    step = pl.program_id(0)

    def forward(near, half):
        base = near * HELD + half * 2 * SUB
        for p in range(SUB):
            reals = pick(core, own[0, 0, half, p], other[0, 0, half, p])
            imags = pick(core, own[0, 1, half, p], other[0, 1, half, p])
            rows = []
            for c in range(2):
                phi = phi_ref[0, 2 * half + c, p]
                rows.append(
                    jnp.concatenate([unfold(phi * reals[c]), unfold(phi * imags[c])], axis=1)
                )
            lines = times_right(jnp.concatenate(rows, axis=0), right.at[Z_FWD])
            first, second = lines[:N], lines[N:]
            field = jnp.concatenate(
                [
                    jnp.concatenate([first[:, :LANES], second[:, :LANES]], axis=1),
                    jnp.concatenate([first[:, LANES:], second[:, LANES:]], axis=1),
                ],
                axis=0,
            )
            spectrum = times_left(left.at[Y_FWD], field)
            for c in range(2):
                at = pl.ds(base + c * SUB + p, N, stride=PLANES)
                lanes = slice(c * LANES, (c + 1) * LANES)
                re_ref[at, :] = spectrum[:N, lanes]
                im_ref[at, :] = spectrum[N:, lanes]

    def middle(block):
        x = lax.broadcasted_iota(jnp.int32, (N, 2 * LANES), 0)
        lane = lax.broadcasted_iota(jnp.int32, (N, 2 * LANES), 1)

        def wave(i):
            return jnp.where(i < N // 2, i, i - N)

        plane = wave(x) ** 2 + wave(lane % LANES) ** 2

        def at(k, ky):
            return pl.ds(pl.multiple_of(k * HELD + ky * PLANES, 8), PLANES)

        for pair in range(LINES // 2):
            ky = block * LINES + 2 * pair
            value = jnp.concatenate(
                [
                    jnp.concatenate([part[at(k, ky), :], part[at(k, ky + 1), :]], axis=1)
                    for part in (re_ref, im_ref)
                    for k in range(4)
                ],
                axis=0,
            )
            square = plane + wave(ky + lane // LANES) ** 2
            weight = jnp.where(square > 0, SCALE / jnp.maximum(square, 1).astype(f32), 0.0)
            spectrum = times_left(left.at[X_FWD], value)
            spectrum = jnp.concatenate([spectrum[:N] * weight, spectrum[N:] * weight], axis=0)
            value = times_left(left.at[X_INV], spectrum)
            for i, part in enumerate((re_ref, im_ref)):
                for k in range(4):
                    first = (4 * i + k) * PLANES
                    for j in range(2):
                        part[at(k, ky + j), :] = value[
                            first : first + PLANES, j * LANES : (j + 1) * LANES
                        ]

    def inverse(near, half):
        base = near * HELD + half * 2 * SUB
        for p in range(SUB):
            loaded = []
            for c in range(2):
                at = pl.ds(base + c * SUB + p, N, stride=PLANES)
                loaded.append((re_ref[at, :], im_ref[at, :]))
            value = jnp.concatenate(
                [
                    jnp.concatenate([loaded[0][0], loaded[1][0]], axis=1),
                    jnp.concatenate([loaded[0][1], loaded[1][1]], axis=1),
                ],
                axis=0,
            )
            value = times_left(left.at[Y_INV], value)
            lines = jnp.concatenate(
                [
                    jnp.concatenate([value[:N, :LANES], value[N:, :LANES]], axis=1),
                    jnp.concatenate([value[:N, LANES:], value[N:, LANES:]], axis=1),
                ],
                axis=0,
            )
            lines = times_right(lines, right.at[Z_INV])
            reals = pick(core, own[0, 0, half, p], other[0, 0, half, p])
            imags = pick(core, own[0, 1, half, p], other[0, 1, half, p])
            terms = []
            for c in range(2):
                real = fold(lines[c * N : (c + 1) * N, :LANES])
                imag = fold(lines[c * N : (c + 1) * N, LANES:])
                at = 2 * half + c
                phi = phi_ref[0, at, p]
                local_ref[at, 0, p] = reals[c] * real + imags[c] * imag
                terms.append((phi * real, phi * imag))
            for r in range(2):
                keep[0, r, half, p] = jnp.where(core == 0, terms[0][r], terms[1][r])
                send[0, r, half, p] = jnp.where(core == 0, terms[1][r], terms[0][r])

    @pl.when(step < FORWARD)
    def _():
        for half in range(2):
            forward(step, half)

    @pl.when((step >= FORWARD) & (step < FORWARD + MIDDLE))
    def _():
        middle(step - FORWARD)

    @pl.when(step >= FORWARD + MIDDLE)
    def _():
        for half in range(2):
            inverse(step - (FORWARD + MIDDLE), half)


def whole(table):
    return pl.BlockSpec(table.shape, lambda *_: (0,) * table.ndim)


def in_place(step):
    return jnp.where(step < FORWARD, step, out_place(step))


def out_place(step):
    return jnp.maximum(step - (FORWARD + MIDDLE), 0)


PIECE = (2, 2, SUB, ROWS, WIDTH)


def solve(ids, phi, own, other):
    tables = [jnp.asarray(RIGHT), jnp.asarray(LEFT)]
    block = (1, 2, 2, SUB, ROWS, WIDTH)

    def phi_at(step, ids):
        return ((ids[1] + in_place(step)) & 3, 0, 0, 0, 0)

    def block_at(step, ids):
        return (in_place(step), 0, 0, 0, 0, 0)

    def term_at(step, ids):
        return (out_place(step), 0, 0, 0, 0, 0)

    def local_at(step, ids):
        return (0, (ids[2] + out_place(step)) & 3, 0, 0, 0)

    return pl.pallas_call(
        field_kernel,
        grid_spec=pltpu.PrefetchScalarGridSpec(
            num_scalar_prefetch=1,
            grid=(FORWARD + MIDDLE + INVERSE,),
            in_specs=[
                pl.BlockSpec((1, 4, SUB, ROWS, WIDTH), phi_at),
                pl.BlockSpec(block, block_at),
                pl.BlockSpec(block, block_at),
            ]
            + [whole(t) for t in tables],
            out_specs=[
                pl.BlockSpec(block, term_at),
                pl.BlockSpec(block, term_at),
                pl.BlockSpec((4, 1, SUB, ROWS, WIDTH), local_at),
            ],
            scratch_shapes=[pltpu.VMEM((4 * HELD, LANES), f32)] * 2,
        ),
        out_shape=[jax.ShapeDtypeStruct((4, *PIECE), f32)] * 2
        + [jax.ShapeDtypeStruct((4, 4, SUB, ROWS, WIDTH), f32)],
        compiler_params=pltpu.CompilerParams(vmem_limit_bytes=48 * 2**20),
        cost_estimate=pl.CostEstimate(
            flops=2 * 3 * 6 * (2 * N) ** 2 * N * N, bytes_accessed=35_000_000, transcendentals=0
        ),
    )(ids, phi, own, other, *tables)


TURN_AXES = ("x_lo", "y", "z", "core")


def turn(value):
    pairs = []
    for a in range(2):
        for y in range(4):
            for z in range(4):
                for c in range(2):
                    source = ((a * 4 + y) * 4 + z) * 2 + c
                    target = ((c * 4 + z) * 4 + y) * 2 + a
                    pairs.append((source, target))
    return lax.ppermute(value, TURN_AXES, pairs)


def other_core(value):
    return lax.ppermute(value, "core", [(0, 1), (1, 0)])


LINE_X = ("x_lo", "x_hi")
RING = {"y": (0, 1, 2, 3), "z": (0, 1, 2, 3), LINE_X: (0, 2, 1, 3)}


def shifted(value, axis, step):
    ring = RING[axis]
    return lax.ppermute(value, axis, [(ring[i], ring[(i + step) % 4]) for i in range(4)])


def ahead(value, axis):
    return shifted(value, axis, 1)


def behind(value, axis):
    return shifted(value, axis, 3)


def halves_of(value):
    size = (value.shape[0] + 1) // 2
    return value[:size], value[size:]


def gather_ring(mine, axis):
    before = ahead(mine, axis)
    after = behind(mine, axis)
    far = ahead(halves_of(before)[0], axis), behind(halves_of(after)[1], axis)
    return jnp.stack([mine, after, jnp.concatenate(far, axis=0), before])


def scatter_ring(parts, axis):
    first, second = halves_of(parts[2])
    first, second = ahead(first, axis), behind(second, axis)
    after, before = halves_of(parts[1]), halves_of(parts[3])
    after = jnp.concatenate([after[0] + first, after[1]], axis=0)
    before = jnp.concatenate([before[0], before[1] + second], axis=0)
    return parts[0] + ahead(after, axis) + behind(before, axis)


def per_device(orbitals, blocks, owner):
    core, y, z = (lax.axis_index(name) for name in ("core", "y", "z"))
    ids = jnp.stack([core, z, (z - y) & 3]).astype(jnp.int32)
    planes = orbitals.shape[1]

    phi = turn(orbitals.reshape(planes, ROWS, WIDTH))
    blocks = blocks.reshape(16, planes, ROWS, WIDTH)
    phi, blocks = lax.optimization_barrier((phi, blocks))
    phi = lax.all_gather(phi, ("y", "x_hi", "x_lo")).reshape(4, 4, planes, ROWS, WIDTH)

    blocks = lax.all_to_all(blocks, ("x_lo", "y", "x_hi"), 0, 0, tiled=True)
    blocks = blocks.reshape(8, 2, planes, ROWS, WIDTH)
    mine = jnp.stack(
        [lax.dynamic_index_in_dim(blocks, owner[r], 0, False) for r in range(ROUNDS)]
    )
    own = gather_ring(mine, "z")
    other = other_core(own)

    keep, send, local = solve(ids, phi, own, other)

    local = lax.psum_scatter(local, ("x_hi", "x_lo"), scatter_dimension=0)
    total = scatter_ring(keep + other_core(send), "z")
    total, local = lax.optimization_barrier((total, local))
    local = scatter_ring(local, "y")
    total = lax.all_to_all(total, "x_hi", 1, 1, tiled=True)
    local = turn(local)
    return (
        local.reshape(1, planes, N * N),
        total.reshape(ROUNDS, 2, planes, N * N),
    )


def solution(mesh):
    fine = Mesh(mesh.devices.reshape(2, 4, 4, 2, 2), ("x_lo", "y", "z", "x_hi", "core"))
    band = ("x_lo", "y")
    grid = ("z", "x_hi", "core")
    return jax.shard_map(
        per_device,
        mesh=fine,
        in_specs=(P(band, grid, None), P(band, grid, None), P()),
        out_specs=(P(band, grid, None), P(None, band, grid, None)),
        check_vma=False,
    )
```

```python
import math

import jax
import jax.numpy as jnp
import ml_dtypes
import numpy as np
from jax import lax
from jax.experimental import pallas as pl
from jax.experimental.pallas import tpu as pltpu
from jax.sharding import Mesh, PartitionSpec as P

N = 96
LANES = 128
FOLD = 4
ROWS = N // FOLD
WIDTH = FOLD * N
ROUNDS = 2
mixing = 0.25
cell_length = 41.04
SCALE = -mixing * 4.0 * math.pi / ((2.0 * math.pi / cell_length) ** 2 * N**3)
f32 = jnp.float32
bf16 = jnp.bfloat16


def trig(rows, columns):
    angle = 2.0 * np.pi * ((rows[:, None] * columns[None, :]) % N) / N
    return np.cos(angle), np.sin(angle)


def two_parts(table):
    high = table.astype(ml_dtypes.bfloat16)
    low = (table - high.astype(np.float64)).astype(ml_dtypes.bfloat16)
    return np.concatenate([high, low], axis=0)


def right_table(sign):
    points = np.arange(N)
    cosine, sine = trig(points, points)
    table = np.zeros((2 * LANES, 2 * LANES))
    table[:N, :N] = cosine
    table[:N, LANES : LANES + N] = sign * sine
    table[LANES : LANES + N, :N] = -sign * sine
    table[LANES : LANES + N, LANES : LANES + N] = cosine
    return two_parts(table)


def left_table(sign, out_points, in_points):
    cosine, sine = trig(out_points, in_points)
    return two_parts(np.block([[cosine, -sign * sine], [sign * sine, cosine]]))


natural = np.arange(N)
folded = (np.arange(N) % ROWS) * FOLD + np.arange(N) // ROWS
RIGHT = np.stack([right_table(-1.0), right_table(1.0)])
Z_FWD, Z_INV = 0, 1
LEFT = np.stack(
    [
        left_table(-1.0, natural, folded),
        left_table(1.0, folded, natural),
        left_table(-1.0, natural, natural),
        left_table(1.0, natural, natural),
    ]
)
Y_FWD, Y_INV, X_FWD, X_INV = 0, 1, 2, 3
SUB = 6
PLANES = 4 * SUB


def split(value):
    high = value.astype(bf16)
    return high, (value - high.astype(f32)).astype(bf16)


def dot(a, b):
    return jnp.dot(a, b, preferred_element_type=f32)


def times_right(value, table):
    high, low = split(value)
    above, below = table[: 2 * LANES, :], table[2 * LANES :, :]
    return dot(high, above) + dot(low, above) + dot(high, below)


def times_left(table, value):
    high, low = split(value)
    first = dot(table[...], high)
    return first[: 2 * N] + first[2 * N :] + dot(table[: 2 * N, :], low)


def unfold(plane):
    lane = lax.broadcasted_iota(jnp.int32, (ROWS, LANES), 1)
    a, b, c = plane[:, :128], plane[:, 128:256], plane[:, 256:]
    return jnp.concatenate(
        [
            a,
            pltpu.roll(jnp.where(lane >= 96, a, b), 32, 1),
            pltpu.roll(jnp.where(lane >= 64, b, c), 64, 1),
            pltpu.roll(c, 96, 1),
        ],
        axis=0,
    )


def fold(field):
    lane = lax.broadcasted_iota(jnp.int32, (ROWS, LANES), 1)
    parts = [field[i * ROWS : (i + 1) * ROWS] for i in range(FOLD)]
    second = pltpu.roll(parts[1], 96, 1)
    third = pltpu.roll(parts[2], 64, 1)
    return jnp.concatenate(
        [
            jnp.where(lane < 96, parts[0], second),
            jnp.where(lane < 64, second, third),
            jnp.where(lane < 32, third, pltpu.roll(parts[3], 32, 1)),
        ],
        axis=1,
    )


def pick(core, own, other):
    first = jnp.where(core == 0, own, other)
    second = jnp.where(core == 0, other, own)
    return first, second


FORWARD = 4
MIDDLE = 2
INVERSE = 4
LINES = N // MIDDLE
HELD = N * PLANES


def field_kernel(
    ids, phi_ref, own, other, own_far, other_far, right, left,
    keep, send, local_ref, re_ref, im_ref
):
    core = ids[0]
    step = pl.program_id(0)

    def block_planes(far, r, half, p):
        mine = jnp.where(far, own_far[r, half, p], own[0, r, half, p])
        theirs = jnp.where(far, other_far[r, half, p], other[0, r, half, p])
        return pick(core, mine, theirs)

    def forward(near, half):
        base = near * HELD + half * 2 * SUB
        for p in range(SUB):
            reals = block_planes(near == FAR, 0, half, p)
            imags = block_planes(near == FAR, 1, half, p)
            rows = []
            for c in range(2):
                phi = phi_ref[0, 2 * half + c, p]
                rows.append(
                    jnp.concatenate([unfold(phi * reals[c]), unfold(phi * imags[c])], axis=1)
                )
            lines = times_right(jnp.concatenate(rows, axis=0), right.at[Z_FWD])
            first, second = lines[:N], lines[N:]
            field = jnp.concatenate(
                [
                    jnp.concatenate([first[:, :LANES], second[:, :LANES]], axis=1),
                    jnp.concatenate([first[:, LANES:], second[:, LANES:]], axis=1),
                ],
                axis=0,
            )
            spectrum = times_left(left.at[Y_FWD], field)
            for c in range(2):
                at = pl.ds(base + c * SUB + p, N, stride=PLANES)
                lanes = slice(c * LANES, (c + 1) * LANES)
                re_ref[at, :] = spectrum[:N, lanes]
                im_ref[at, :] = spectrum[N:, lanes]

    def middle(block):
        x = lax.broadcasted_iota(jnp.int32, (N, 2 * LANES), 0)
        lane = lax.broadcasted_iota(jnp.int32, (N, 2 * LANES), 1)

        def wave(i):
            return jnp.where(i < N // 2, i, i - N)

        plane = wave(x) ** 2 + wave(lane % LANES) ** 2

        def at(k, ky):
            return pl.ds(pl.multiple_of(k * HELD + ky * PLANES, 8), PLANES)

        for pair in range(LINES // 2):
            ky = block * LINES + 2 * pair
            value = jnp.concatenate(
                [
                    jnp.concatenate([part[at(k, ky), :], part[at(k, ky + 1), :]], axis=1)
                    for part in (re_ref, im_ref)
                    for k in range(4)
                ],
                axis=0,
            )
            square = plane + wave(ky + lane // LANES) ** 2
            weight = jnp.where(square > 0, SCALE / jnp.maximum(square, 1).astype(f32), 0.0)
            spectrum = times_left(left.at[X_FWD], value)
            spectrum = jnp.concatenate([spectrum[:N] * weight, spectrum[N:] * weight], axis=0)
            value = times_left(left.at[X_INV], spectrum)
            for i, part in enumerate((re_ref, im_ref)):
                for k in range(4):
                    first = (4 * i + k) * PLANES
                    for j in range(2):
                        part[at(k, ky + j), :] = value[
                            first : first + PLANES, j * LANES : (j + 1) * LANES
                        ]

    def inverse(near, half):
        base = near * HELD + half * 2 * SUB
        for p in range(SUB):
            loaded = []
            for c in range(2):
                at = pl.ds(base + c * SUB + p, N, stride=PLANES)
                loaded.append((re_ref[at, :], im_ref[at, :]))
            value = jnp.concatenate(
                [
                    jnp.concatenate([loaded[0][0], loaded[1][0]], axis=1),
                    jnp.concatenate([loaded[0][1], loaded[1][1]], axis=1),
                ],
                axis=0,
            )
            value = times_left(left.at[Y_INV], value)
            lines = jnp.concatenate(
                [
                    jnp.concatenate([value[:N, :LANES], value[N:, :LANES]], axis=1),
                    jnp.concatenate([value[:N, LANES:], value[N:, LANES:]], axis=1),
                ],
                axis=0,
            )
            lines = times_right(lines, right.at[Z_INV])
            reals = block_planes(near == FAR, 0, half, p)
            imags = block_planes(near == FAR, 1, half, p)
            terms = []
            for c in range(2):
                real = fold(lines[c * N : (c + 1) * N, :LANES])
                imag = fold(lines[c * N : (c + 1) * N, LANES:])
                at = 2 * half + c
                phi = phi_ref[0, at, p]
                local_ref[at, 0, p] = reals[c] * real + imags[c] * imag
                terms.append((phi * real, phi * imag))
            for r in range(2):
                keep[0, r, half, p] = jnp.where(core == 0, terms[0][r], terms[1][r])
                send[0, r, half, p] = jnp.where(core == 0, terms[1][r], terms[0][r])

    @pl.when(step < FORWARD)
    def _():
        for half in range(2):
            forward(in_place(step), half)

    @pl.when((step >= FORWARD) & (step < FORWARD + MIDDLE))
    def _():
        middle(step - FORWARD)

    @pl.when(step >= FORWARD + MIDDLE)
    def _():
        for half in range(2):
            inverse(out_place(step), half)


def whole(table):
    return pl.BlockSpec(table.shape, lambda *_: (0,) * table.ndim)


FAR = 2


def order(step):
    return step ^ (step >> 1)


def in_step(step):
    return jnp.where(step < FORWARD, step, out_step(step))


def out_step(step):
    return jnp.maximum(step - (FORWARD + MIDDLE), 0)


def in_place(step):
    return order(in_step(step))


def out_place(step):
    return order(out_step(step))


PIECE = (2, 2, SUB, ROWS, WIDTH)


def solve(ids, phi, own, other, own_far, other_far):
    tables = [jnp.asarray(RIGHT), jnp.asarray(LEFT)]
    block = (1, 2, 2, SUB, ROWS, WIDTH)

    def phi_at(step, ids):
        return ((ids[1] + in_place(step)) & 3, 0, 0, 0, 0)

    def block_at(step, ids):
        return (jnp.minimum(in_step(step), 2), 0, 0, 0, 0, 0)

    def term_at(step, ids):
        return (out_place(step), 0, 0, 0, 0, 0)

    def local_at(step, ids):
        return (0, (ids[2] + out_place(step)) & 3, 0, 0, 0)

    return pl.pallas_call(
        field_kernel,
        grid_spec=pltpu.PrefetchScalarGridSpec(
            num_scalar_prefetch=1,
            grid=(FORWARD + MIDDLE + INVERSE,),
            in_specs=[
                pl.BlockSpec((1, 4, SUB, ROWS, WIDTH), phi_at),
                pl.BlockSpec(block, block_at),
                pl.BlockSpec(block, block_at),
                whole(own_far),
                whole(other_far),
            ]
            + [whole(t) for t in tables],
            out_specs=[
                pl.BlockSpec(block, term_at),
                pl.BlockSpec(block, term_at),
                pl.BlockSpec((4, 1, SUB, ROWS, WIDTH), local_at),
            ],
            scratch_shapes=[pltpu.VMEM((4 * HELD + PLANES, LANES), f32)] * 2,
        ),
        out_shape=[jax.ShapeDtypeStruct((4, *PIECE), f32)] * 2
        + [jax.ShapeDtypeStruct((4, 4, SUB, ROWS, WIDTH), f32)],
        compiler_params=pltpu.CompilerParams(vmem_limit_bytes=48 * 2**20),
        cost_estimate=pl.CostEstimate(
            flops=2 * 3 * 6 * (2 * N) ** 2 * N * N, bytes_accessed=35_000_000, transcendentals=0
        ),
    )(ids, phi, own, other, own_far, other_far, *tables)


TURN_AXES = ("x_lo", "y", "z", "core")


def turn(value):
    pairs = []
    for a in range(2):
        for y in range(4):
            for z in range(4):
                for c in range(2):
                    source = ((a * 4 + y) * 4 + z) * 2 + c
                    target = ((c * 4 + z) * 4 + y) * 2 + a
                    pairs.append((source, target))
    return lax.ppermute(value, TURN_AXES, pairs)


def other_core(value):
    return lax.ppermute(value, "core", [(0, 1), (1, 0)])


LINE_X = ("x_lo", "x_hi")
RING = {"y": (0, 1, 2, 3), "z": (0, 1, 2, 3), LINE_X: (0, 2, 1, 3)}


def shifted(value, axis, step):
    ring = RING[axis]
    return lax.ppermute(value, axis, [(ring[i], ring[(i + step) % 4]) for i in range(4)])


def ahead(value, axis):
    return shifted(value, axis, 1)


def behind(value, axis):
    return shifted(value, axis, 3)


def halves_of(value):
    size = (value.shape[0] + 1) // 2
    return value[:size], value[size:]


def gather_ring(mine, axis):
    before = ahead(mine, axis)
    after = behind(mine, axis)
    far = ahead(halves_of(before)[0], axis), behind(halves_of(after)[1], axis)
    return jnp.stack([mine, after, before]), jnp.concatenate(far, axis=0)


def scatter_ring(parts, axis):
    first, second = halves_of(parts[2])
    first, second = ahead(first, axis), behind(second, axis)
    after, before = halves_of(parts[1]), halves_of(parts[3])
    after = jnp.concatenate([after[0] + first, after[1]], axis=0)
    before = jnp.concatenate([before[0], before[1] + second], axis=0)
    return parts[0] + ahead(after, axis) + behind(before, axis)


def per_device(orbitals, blocks, owner):
    core, y, z = (lax.axis_index(name) for name in ("core", "y", "z"))
    ids = jnp.stack([core, z, (z - y) & 3]).astype(jnp.int32)
    planes = orbitals.shape[1]

    phi = turn(orbitals.reshape(planes, ROWS, WIDTH))
    blocks = blocks.reshape(16, planes, ROWS, WIDTH)
    phi, blocks = lax.optimization_barrier((phi, blocks))
    phi = lax.all_gather(phi, ("y", "x_hi", "x_lo")).reshape(4, 4, planes, ROWS, WIDTH)

    blocks = lax.all_to_all(blocks, ("x_lo", "y", "x_hi"), 0, 0, tiled=True)
    blocks = blocks.reshape(8, 2, planes, ROWS, WIDTH)
    mine = jnp.stack(
        [lax.dynamic_index_in_dim(blocks, owner[r], 0, False) for r in range(ROUNDS)]
    )
    own, own_far = gather_ring(mine, "z")
    other, other_far = other_core(own), other_core(own_far)

    keep, send, local = solve(ids, phi, own, other, own_far, other_far)

    local = lax.psum_scatter(local, ("x_hi", "x_lo"), scatter_dimension=0)
    total = scatter_ring(keep + other_core(send), "z")
    total, local = lax.optimization_barrier((total, local))
    local = scatter_ring(local, "y")
    total = lax.all_to_all(total, "x_hi", 1, 1, tiled=True)
    local = turn(local)
    return (
        local.reshape(1, planes, N * N),
        total.reshape(ROUNDS, 2, planes, N * N),
    )


def solution(mesh):
    fine = Mesh(mesh.devices.reshape(2, 4, 4, 2, 2), ("x_lo", "y", "z", "x_hi", "core"))
    band = ("x_lo", "y")
    grid = ("z", "x_hi", "core")
    return jax.shard_map(
        per_device,
        mesh=fine,
        in_specs=(P(band, grid, None), P(band, grid, None), P()),
        out_specs=(P(band, grid, None), P(None, band, grid, None)),
        check_vma=False,
    )
```

```python
import math

import jax
import jax.numpy as jnp
import ml_dtypes
import numpy as np
from jax import lax
from jax.experimental import pallas as pl
from jax.experimental.pallas import tpu as pltpu
from jax.sharding import Mesh, PartitionSpec as P

N = 96
LANES = 128
FOLD = 4
ROWS = N // FOLD
WIDTH = FOLD * N
ROUNDS = 2
mixing = 0.25
cell_length = 41.04
SCALE = -mixing * 4.0 * math.pi / ((2.0 * math.pi / cell_length) ** 2 * N**3)
f32 = jnp.float32
bf16 = jnp.bfloat16


def trig(rows, columns):
    angle = 2.0 * np.pi * ((rows[:, None] * columns[None, :]) % N) / N
    return np.cos(angle), np.sin(angle)


def two_parts(table):
    high = table.astype(ml_dtypes.bfloat16)
    low = (table - high.astype(np.float64)).astype(ml_dtypes.bfloat16)
    return np.concatenate([high, low], axis=0)


def right_table(sign):
    points = np.arange(N)
    cosine, sine = trig(points, points)
    table = np.zeros((2 * LANES, 2 * LANES))
    table[:N, :N] = cosine
    table[:N, LANES : LANES + N] = sign * sine
    table[LANES : LANES + N, :N] = -sign * sine
    table[LANES : LANES + N, LANES : LANES + N] = cosine
    return two_parts(table)


def left_table(sign, out_points, in_points):
    cosine, sine = trig(out_points, in_points)
    return two_parts(np.block([[cosine, -sign * sine], [sign * sine, cosine]]))


natural = np.arange(N)
folded = (np.arange(N) % ROWS) * FOLD + np.arange(N) // ROWS
RIGHT = np.stack([right_table(-1.0), right_table(1.0)])
Z_FWD, Z_INV = 0, 1
LEFT = np.stack(
    [
        left_table(-1.0, natural, folded),
        left_table(1.0, folded, natural),
        left_table(-1.0, natural, natural),
        left_table(1.0, natural, natural),
    ]
)
Y_FWD, Y_INV, X_FWD, X_INV = 0, 1, 2, 3
SUB = 6
PLANES = 4 * SUB


def split(value):
    high = value.astype(bf16)
    return high, (value - high.astype(f32)).astype(bf16)


def dot(a, b):
    return jnp.dot(a, b, preferred_element_type=f32)


def times_right(value, table):
    high, low = split(value)
    above, below = table[: 2 * LANES, :], table[2 * LANES :, :]
    return dot(high, above) + dot(low, above) + dot(high, below)


def times_left(table, value):
    high, low = split(value)
    first = dot(table[...], high)
    return first[: 2 * N] + first[2 * N :] + dot(table[: 2 * N, :], low)


def unfold(plane):
    lane = lax.broadcasted_iota(jnp.int32, (ROWS, LANES), 1)
    a, b, c = plane[:, :128], plane[:, 128:256], plane[:, 256:]
    return jnp.concatenate(
        [
            a,
            pltpu.roll(jnp.where(lane >= 96, a, b), 32, 1),
            pltpu.roll(jnp.where(lane >= 64, b, c), 64, 1),
            pltpu.roll(c, 96, 1),
        ],
        axis=0,
    )


def fold(field):
    lane = lax.broadcasted_iota(jnp.int32, (ROWS, LANES), 1)
    parts = [field[i * ROWS : (i + 1) * ROWS] for i in range(FOLD)]
    second = pltpu.roll(parts[1], 96, 1)
    third = pltpu.roll(parts[2], 64, 1)
    return jnp.concatenate(
        [
            jnp.where(lane < 96, parts[0], second),
            jnp.where(lane < 64, second, third),
            jnp.where(lane < 32, third, pltpu.roll(parts[3], 32, 1)),
        ],
        axis=1,
    )


def pick(core, own, other):
    first = jnp.where(core == 0, own, other)
    second = jnp.where(core == 0, other, own)
    return first, second


FORWARD = 4
MIDDLE = 2
INVERSE = 4
LINES = N // MIDDLE
HELD = N * PLANES


def field_kernel(
    ids, phi_ref, own, other, own_far, other_far, right, left,
    keep, send, local_ref, re_ref, im_ref
):
    core = ids[0]
    step = pl.program_id(0)

    def block_planes(far, r, half, p):
        mine = jnp.where(far, own_far[r, half, p], own[0, r, half, p])
        theirs = jnp.where(far, other_far[r, half, p], other[0, r, half, p])
        return pick(core, mine, theirs)

    def forward(near, half):
        base = near * HELD + half * 2 * SUB
        for p in range(SUB):
            reals = block_planes(near == FAR, 0, half, p)
            imags = block_planes(near == FAR, 1, half, p)
            rows = []
            for c in range(2):
                phi = phi_ref[0, 2 * half + c, p]
                rows.append(
                    jnp.concatenate([unfold(phi * reals[c]), unfold(phi * imags[c])], axis=1)
                )
            lines = times_right(jnp.concatenate(rows, axis=0), right.at[Z_FWD])
            first, second = lines[:N], lines[N:]
            field = jnp.concatenate(
                [
                    jnp.concatenate([first[:, :LANES], second[:, :LANES]], axis=1),
                    jnp.concatenate([first[:, LANES:], second[:, LANES:]], axis=1),
                ],
                axis=0,
            )
            spectrum = times_left(left.at[Y_FWD], field)
            for c in range(2):
                at = pl.ds(base + c * SUB + p, N, stride=PLANES)
                lanes = slice(c * LANES, (c + 1) * LANES)
                re_ref[at, :] = spectrum[:N, lanes]
                im_ref[at, :] = spectrum[N:, lanes]

    def middle(block):
        x = lax.broadcasted_iota(jnp.int32, (N, 2 * LANES), 0)
        lane = lax.broadcasted_iota(jnp.int32, (N, 2 * LANES), 1)

        def wave(i):
            return jnp.where(i < N // 2, i, i - N)

        plane = wave(x) ** 2 + wave(lane % LANES) ** 2

        def at(k, ky):
            return pl.ds(pl.multiple_of(k * HELD + ky * PLANES, 8), PLANES)

        for pair in range(LINES // 2):
            ky = block * LINES + 2 * pair
            value = jnp.concatenate(
                [
                    jnp.concatenate([part[at(k, ky), :], part[at(k, ky + 1), :]], axis=1)
                    for part in (re_ref, im_ref)
                    for k in range(4)
                ],
                axis=0,
            )
            square = plane + wave(ky + lane // LANES) ** 2
            weight = jnp.where(square > 0, SCALE / jnp.maximum(square, 1).astype(f32), 0.0)
            spectrum = times_left(left.at[X_FWD], value)
            spectrum = jnp.concatenate([spectrum[:N] * weight, spectrum[N:] * weight], axis=0)
            value = times_left(left.at[X_INV], spectrum)
            for i, part in enumerate((re_ref, im_ref)):
                for k in range(4):
                    first = (4 * i + k) * PLANES
                    for j in range(2):
                        part[at(k, ky + j), :] = value[
                            first : first + PLANES, j * LANES : (j + 1) * LANES
                        ]

    def inverse(near, half):
        base = near * HELD + half * 2 * SUB
        for p in range(SUB):
            loaded = []
            for c in range(2):
                at = pl.ds(base + c * SUB + p, N, stride=PLANES)
                loaded.append((re_ref[at, :], im_ref[at, :]))
            value = jnp.concatenate(
                [
                    jnp.concatenate([loaded[0][0], loaded[1][0]], axis=1),
                    jnp.concatenate([loaded[0][1], loaded[1][1]], axis=1),
                ],
                axis=0,
            )
            value = times_left(left.at[Y_INV], value)
            lines = jnp.concatenate(
                [
                    jnp.concatenate([value[:N, :LANES], value[N:, :LANES]], axis=1),
                    jnp.concatenate([value[:N, LANES:], value[N:, LANES:]], axis=1),
                ],
                axis=0,
            )
            lines = times_right(lines, right.at[Z_INV])
            reals = block_planes(near == FAR, 0, half, p)
            imags = block_planes(near == FAR, 1, half, p)
            terms = []
            for c in range(2):
                real = fold(lines[c * N : (c + 1) * N, :LANES])
                imag = fold(lines[c * N : (c + 1) * N, LANES:])
                at = 2 * half + c
                phi = phi_ref[0, at, p]
                local_ref[at, 0, p] = reals[c] * real + imags[c] * imag
                terms.append((phi * real, phi * imag))
            for r in range(2):
                keep[0, r, half, p] = jnp.where(core == 0, terms[0][r], terms[1][r])
                send[0, r, half, p] = jnp.where(core == 0, terms[1][r], terms[0][r])

    @pl.when(step < FORWARD)
    def _():
        for half in range(2):
            forward(in_place(step), half)

    @pl.when((step >= FORWARD) & (step < FORWARD + MIDDLE))
    def _():
        middle(step - FORWARD)

    @pl.when(step >= FORWARD + MIDDLE)
    def _():
        for half in range(2):
            inverse(out_place(step), half)


def whole(table):
    return pl.BlockSpec(table.shape, lambda *_: (0,) * table.ndim)


FAR = 2


def order(step):
    return step ^ (step >> 1)


def in_step(step):
    return jnp.where(step < FORWARD, step, out_step(step))


def out_step(step):
    return jnp.maximum(step - (FORWARD + MIDDLE), 0)


def in_place(step):
    return order(in_step(step))


def out_place(step):
    return order(out_step(step))


PIECE = (2, 2, SUB, ROWS, WIDTH)


def solve(ids, phi, own, other, own_far, other_far):
    tables = [jnp.asarray(RIGHT), jnp.asarray(LEFT)]
    block = (1, 2, 2, SUB, ROWS, WIDTH)

    def phi_at(step, ids):
        return ((ids[1] + in_place(step)) & 3, 0, 0, 0, 0)

    def block_at(step, ids):
        return (jnp.minimum(in_step(step), 2), 0, 0, 0, 0, 0)

    def term_at(step, ids):
        return (out_place(step), 0, 0, 0, 0, 0)

    def local_at(step, ids):
        return (0, (ids[2] + out_place(step)) & 3, 0, 0, 0)

    return pl.pallas_call(
        field_kernel,
        grid_spec=pltpu.PrefetchScalarGridSpec(
            num_scalar_prefetch=1,
            grid=(FORWARD + MIDDLE + INVERSE,),
            in_specs=[
                pl.BlockSpec((1, 4, SUB, ROWS, WIDTH), phi_at),
                pl.BlockSpec(block, block_at),
                pl.BlockSpec(block, block_at),
                whole(own_far),
                whole(other_far),
            ]
            + [whole(t) for t in tables],
            out_specs=[
                pl.BlockSpec(block, term_at),
                pl.BlockSpec(block, term_at),
                pl.BlockSpec((4, 1, SUB, ROWS, WIDTH), local_at),
            ],
            scratch_shapes=[pltpu.VMEM((4 * HELD + PLANES, LANES), f32)] * 2,
        ),
        out_shape=[jax.ShapeDtypeStruct((4, *PIECE), f32)] * 2
        + [jax.ShapeDtypeStruct((4, 4, SUB, ROWS, WIDTH), f32)],
        compiler_params=pltpu.CompilerParams(vmem_limit_bytes=48 * 2**20),
        cost_estimate=pl.CostEstimate(
            flops=2 * 3 * 6 * (2 * N) ** 2 * N * N, bytes_accessed=35_000_000, transcendentals=0
        ),
    )(ids, phi, own, other, own_far, other_far, *tables)


TURN_AXES = ("x_lo", "y", "z", "core")


def turn(value):
    pairs = []
    for a in range(2):
        for y in range(4):
            for z in range(4):
                for c in range(2):
                    source = ((a * 4 + y) * 4 + z) * 2 + c
                    target = ((c * 4 + z) * 4 + y) * 2 + a
                    pairs.append((source, target))
    return lax.ppermute(value, TURN_AXES, pairs)


def other_core(value):
    return lax.ppermute(value, "core", [(0, 1), (1, 0)])


LINE_X = ("x_lo", "x_hi")
RING = {"y": (0, 1, 2, 3), "z": (0, 1, 2, 3), LINE_X: (0, 2, 1, 3)}


def shifted(value, axis, step):
    ring = RING[axis]
    return lax.ppermute(value, axis, [(ring[i], ring[(i + step) % 4]) for i in range(4)])


def ahead(value, axis):
    return shifted(value, axis, 1)


def behind(value, axis):
    return shifted(value, axis, 3)


def halves_of(value):
    size = (value.shape[0] + 1) // 2
    return value[:size], value[size:]


def gather_ring(mine, axis):
    before = ahead(mine, axis)
    after = behind(mine, axis)
    far = ahead(halves_of(before)[0], axis), behind(halves_of(after)[1], axis)
    return jnp.stack([mine, after, before]), jnp.concatenate(far, axis=0)


def scatter_ring(parts, axis):
    first, second = halves_of(parts[2])
    first, second = ahead(first, axis), behind(second, axis)
    after, before = halves_of(parts[1]), halves_of(parts[3])
    after = jnp.concatenate([after[0] + first, after[1]], axis=0)
    before = jnp.concatenate([before[0], before[1] + second], axis=0)
    return parts[0] + ahead(after, axis) + behind(before, axis)


def per_device(orbitals, blocks, owner):
    core, y, z = (lax.axis_index(name) for name in ("core", "y", "z"))
    ids = jnp.stack([core, z, (z - y) & 3]).astype(jnp.int32)
    planes = orbitals.shape[1]

    phi = turn(orbitals.reshape(planes, ROWS, WIDTH))
    blocks = blocks.reshape(16, planes, ROWS, WIDTH)
    phi, blocks = lax.optimization_barrier((phi, blocks))
    phi = lax.all_gather(phi, ("y", "x_hi", "x_lo")).reshape(4, 4, planes, ROWS, WIDTH)

    blocks = lax.all_to_all(blocks, ("x_lo", "y", "x_hi"), 0, 0, tiled=True)
    blocks = blocks.reshape(8, 2, planes, ROWS, WIDTH)
    mine = jnp.stack(
        [lax.dynamic_index_in_dim(blocks, owner[r], 0, False) for r in range(ROUNDS)]
    )
    own, own_far = gather_ring(mine, "z")
    other, other_far = other_core(own), other_core(own_far)

    keep, send, local = solve(ids, phi, own, other, own_far, other_far)

    local = lax.psum_scatter(local, ("x_hi", "x_lo"), scatter_dimension=0)
    total = scatter_ring(keep + other_core(send), "z")
    total, local = lax.optimization_barrier((total, local))
    local = local[0] + sum(shifted(local[k], "y", k) for k in (1, 2, 3))
    total = lax.all_to_all(total, "x_hi", 1, 1, tiled=True)
    local = turn(local)
    return (
        local.reshape(1, planes, N * N),
        total.reshape(ROUNDS, 2, planes, N * N),
    )


def solution(mesh):
    fine = Mesh(mesh.devices.reshape(2, 4, 4, 2, 2), ("x_lo", "y", "z", "x_hi", "core"))
    band = ("x_lo", "y")
    grid = ("z", "x_hi", "core")
    return jax.shard_map(
        per_device,
        mesh=fine,
        in_specs=(P(band, grid, None), P(band, grid, None), P()),
        out_specs=(P(band, grid, None), P(None, band, grid, None)),
        check_vma=False,
    )
```

```python
import math

import jax
import jax.numpy as jnp
import ml_dtypes
import numpy as np
from jax import lax
from jax.experimental import pallas as pl
from jax.experimental.pallas import tpu as pltpu
from jax.sharding import Mesh, PartitionSpec as P

N = 96
LANES = 128
FOLD = 4
ROWS = N // FOLD
WIDTH = FOLD * N
ROUNDS = 2
mixing = 0.25
cell_length = 41.04
SCALE = -mixing * 4.0 * math.pi / ((2.0 * math.pi / cell_length) ** 2 * N**3)
f32 = jnp.float32
bf16 = jnp.bfloat16


def trig(rows, columns):
    angle = 2.0 * np.pi * ((rows[:, None] * columns[None, :]) % N) / N
    return np.cos(angle), np.sin(angle)


def two_parts(table):
    high = table.astype(ml_dtypes.bfloat16)
    low = (table - high.astype(np.float64)).astype(ml_dtypes.bfloat16)
    return np.concatenate([high, low], axis=0)


def right_table(sign):
    points = np.arange(N)
    cosine, sine = trig(points, points)
    table = np.zeros((2 * LANES, 2 * LANES))
    table[:N, :N] = cosine
    table[:N, LANES : LANES + N] = sign * sine
    table[LANES : LANES + N, :N] = -sign * sine
    table[LANES : LANES + N, LANES : LANES + N] = cosine
    return two_parts(table)


def left_table(sign, out_points, in_points):
    cosine, sine = trig(out_points, in_points)
    return two_parts(np.block([[cosine, -sign * sine], [sign * sine, cosine]]))


natural = np.arange(N)
folded = (np.arange(N) % ROWS) * FOLD + np.arange(N) // ROWS
RIGHT = np.stack([right_table(-1.0), right_table(1.0)])
Z_FWD, Z_INV = 0, 1
LEFT = np.stack(
    [
        left_table(-1.0, natural, folded),
        left_table(1.0, folded, natural),
        left_table(-1.0, natural, natural),
        left_table(1.0, natural, natural),
    ]
)
Y_FWD, Y_INV, X_FWD, X_INV = 0, 1, 2, 3
SUB = 6
PLANES = 4 * SUB


def split(value):
    high = value.astype(bf16)
    return high, (value - high.astype(f32)).astype(bf16)


def dot(a, b):
    return jnp.dot(a, b, preferred_element_type=f32)


def times_right(value, table):
    high, low = split(value)
    above, below = table[: 2 * LANES, :], table[2 * LANES :, :]
    return dot(high, above) + dot(low, above) + dot(high, below)


def times_left(table, value):
    high, low = split(value)
    first = dot(table[...], high)
    return first[: 2 * N] + first[2 * N :] + dot(table[: 2 * N, :], low)


def unfold(plane):
    lane = lax.broadcasted_iota(jnp.int32, (ROWS, LANES), 1)
    a, b, c = plane[:, :128], plane[:, 128:256], plane[:, 256:]
    return jnp.concatenate(
        [
            a,
            pltpu.roll(jnp.where(lane >= 96, a, b), 32, 1),
            pltpu.roll(jnp.where(lane >= 64, b, c), 64, 1),
            pltpu.roll(c, 96, 1),
        ],
        axis=0,
    )


def fold(field):
    lane = lax.broadcasted_iota(jnp.int32, (ROWS, LANES), 1)
    parts = [field[i * ROWS : (i + 1) * ROWS] for i in range(FOLD)]
    second = pltpu.roll(parts[1], 96, 1)
    third = pltpu.roll(parts[2], 64, 1)
    return jnp.concatenate(
        [
            jnp.where(lane < 96, parts[0], second),
            jnp.where(lane < 64, second, third),
            jnp.where(lane < 32, third, pltpu.roll(parts[3], 32, 1)),
        ],
        axis=1,
    )


def pick(core, own, other):
    first = jnp.where(core == 0, own, other)
    second = jnp.where(core == 0, other, own)
    return first, second


FORWARD = 4
MIDDLE = 2
INVERSE = 4
LINES = N // MIDDLE
HELD = N * PLANES


def field_kernel(
    ids, phi_ref, own, other, own_far, other_far, right, left,
    keep, send, local_ref, re_ref, im_ref
):
    core = ids[0]
    step = pl.program_id(0)

    def block_planes(far, r, half, p):
        mine = jnp.where(far, own_far[r, half, p], own[0, r, half, p])
        theirs = jnp.where(far, other_far[r, half, p], other[0, r, half, p])
        return pick(core, mine, theirs)

    def forward(near, half):
        base = near * HELD + half * 2 * SUB
        for p in range(SUB):
            reals = block_planes(near == FAR, 0, half, p)
            imags = block_planes(near == FAR, 1, half, p)
            rows = []
            for c in range(2):
                phi = phi_ref[0, 2 * half + c, p]
                rows.append(
                    jnp.concatenate([unfold(phi * reals[c]), unfold(phi * imags[c])], axis=1)
                )
            lines = times_right(jnp.concatenate(rows, axis=0), right.at[Z_FWD])
            first, second = lines[:N], lines[N:]
            field = jnp.concatenate(
                [
                    jnp.concatenate([first[:, :LANES], second[:, :LANES]], axis=1),
                    jnp.concatenate([first[:, LANES:], second[:, LANES:]], axis=1),
                ],
                axis=0,
            )
            spectrum = times_left(left.at[Y_FWD], field)
            for c in range(2):
                at = pl.ds(base + c * SUB + p, N, stride=PLANES)
                lanes = slice(c * LANES, (c + 1) * LANES)
                re_ref[at, :] = spectrum[:N, lanes]
                im_ref[at, :] = spectrum[N:, lanes]

    def middle(block):
        x = lax.broadcasted_iota(jnp.int32, (N, 2 * LANES), 0)
        lane = lax.broadcasted_iota(jnp.int32, (N, 2 * LANES), 1)

        def wave(i):
            return jnp.where(i < N // 2, i, i - N)

        plane = wave(x) ** 2 + wave(lane % LANES) ** 2

        def at(k, ky):
            return pl.ds(pl.multiple_of(k * HELD + ky * PLANES, 8), PLANES)

        for pair in range(LINES // 2):
            ky = block * LINES + 2 * pair
            value = jnp.concatenate(
                [
                    jnp.concatenate([part[at(k, ky), :], part[at(k, ky + 1), :]], axis=1)
                    for part in (re_ref, im_ref)
                    for k in range(4)
                ],
                axis=0,
            )
            square = plane + wave(ky + lane // LANES) ** 2
            weight = jnp.where(square > 0, SCALE / jnp.maximum(square, 1).astype(f32), 0.0)
            spectrum = times_left(left.at[X_FWD], value)
            spectrum = jnp.concatenate([spectrum[:N] * weight, spectrum[N:] * weight], axis=0)
            value = times_left(left.at[X_INV], spectrum)
            for i, part in enumerate((re_ref, im_ref)):
                for k in range(4):
                    first = (4 * i + k) * PLANES
                    for j in range(2):
                        part[at(k, ky + j), :] = value[
                            first : first + PLANES, j * LANES : (j + 1) * LANES
                        ]

    def inverse(near, half):
        base = near * HELD + half * 2 * SUB
        for p in range(SUB):
            loaded = []
            for c in range(2):
                at = pl.ds(base + c * SUB + p, N, stride=PLANES)
                loaded.append((re_ref[at, :], im_ref[at, :]))
            value = jnp.concatenate(
                [
                    jnp.concatenate([loaded[0][0], loaded[1][0]], axis=1),
                    jnp.concatenate([loaded[0][1], loaded[1][1]], axis=1),
                ],
                axis=0,
            )
            value = times_left(left.at[Y_INV], value)
            lines = jnp.concatenate(
                [
                    jnp.concatenate([value[:N, :LANES], value[N:, :LANES]], axis=1),
                    jnp.concatenate([value[:N, LANES:], value[N:, LANES:]], axis=1),
                ],
                axis=0,
            )
            lines = times_right(lines, right.at[Z_INV])
            reals = block_planes(near == FAR, 0, half, p)
            imags = block_planes(near == FAR, 1, half, p)
            terms = []
            for c in range(2):
                real = fold(lines[c * N : (c + 1) * N, :LANES])
                imag = fold(lines[c * N : (c + 1) * N, LANES:])
                at = 2 * half + c
                phi = phi_ref[0, at, p]
                local_ref[at, 0, p] = reals[c] * real + imags[c] * imag
                terms.append((phi * real, phi * imag))
            for r in range(2):
                keep[0, r, half, p] = jnp.where(core == 0, terms[0][r], terms[1][r])
                send[0, r, half, p] = jnp.where(core == 0, terms[1][r], terms[0][r])

    @pl.when(step < FORWARD)
    def _():
        for half in range(2):
            forward(in_place(step), half)

    @pl.when((step >= FORWARD) & (step < FORWARD + MIDDLE))
    def _():
        middle(step - FORWARD)

    @pl.when(step >= FORWARD + MIDDLE)
    def _():
        for half in range(2):
            inverse(out_place(step), half)


def whole(table):
    return pl.BlockSpec(table.shape, lambda *_: (0,) * table.ndim)


FAR = 2


def order(step):
    return step ^ (step >> 1)


def in_step(step):
    return jnp.where(step < FORWARD, step, out_step(step))


def out_step(step):
    return jnp.maximum(step - (FORWARD + MIDDLE), 0)


def in_place(step):
    return order(in_step(step))


def out_place(step):
    return order(out_step(step))


PIECE = (2, 2, SUB, ROWS, WIDTH)


def solve(ids, phi, own, other, own_far, other_far):
    tables = [jnp.asarray(RIGHT), jnp.asarray(LEFT)]
    block = (1, 2, 2, SUB, ROWS, WIDTH)

    def phi_at(step, ids):
        return ((ids[1] + in_place(step)) & 3, 0, 0, 0, 0)

    def block_at(step, ids):
        return (jnp.minimum(in_step(step), 2), 0, 0, 0, 0, 0)

    def term_at(step, ids):
        return (out_place(step), 0, 0, 0, 0, 0)

    def local_at(step, ids):
        return (0, (ids[2] + out_place(step)) & 3, 0, 0, 0)

    return pl.pallas_call(
        field_kernel,
        grid_spec=pltpu.PrefetchScalarGridSpec(
            num_scalar_prefetch=1,
            grid=(FORWARD + MIDDLE + INVERSE,),
            in_specs=[
                pl.BlockSpec((1, 4, SUB, ROWS, WIDTH), phi_at),
                pl.BlockSpec(block, block_at),
                pl.BlockSpec(block, block_at),
                whole(own_far),
                whole(other_far),
            ]
            + [whole(t) for t in tables],
            out_specs=[
                pl.BlockSpec(block, term_at),
                pl.BlockSpec(block, term_at),
                pl.BlockSpec((4, 1, SUB, ROWS, WIDTH), local_at),
            ],
            scratch_shapes=[pltpu.VMEM((4 * HELD + PLANES, LANES), f32)] * 2,
        ),
        out_shape=[jax.ShapeDtypeStruct((4, *PIECE), f32)] * 2
        + [jax.ShapeDtypeStruct((4, 4, SUB, ROWS, WIDTH), f32)],
        compiler_params=pltpu.CompilerParams(vmem_limit_bytes=48 * 2**20),
        cost_estimate=pl.CostEstimate(
            flops=2 * 3 * 6 * (2 * N) ** 2 * N * N, bytes_accessed=35_000_000, transcendentals=0
        ),
    )(ids, phi, own, other, own_far, other_far, *tables)


TURN_AXES = ("x_lo", "y", "z", "core")


def turn(value):
    pairs = []
    for a in range(2):
        for y in range(4):
            for z in range(4):
                for c in range(2):
                    source = ((a * 4 + y) * 4 + z) * 2 + c
                    target = ((c * 4 + z) * 4 + y) * 2 + a
                    pairs.append((source, target))
    return lax.ppermute(value, TURN_AXES, pairs)


def other_core(value):
    return lax.ppermute(value, "core", [(0, 1), (1, 0)])


LINE_X = ("x_lo", "x_hi")
RING = {"y": (0, 1, 2, 3), "z": (0, 1, 2, 3), LINE_X: (0, 2, 1, 3)}


def shifted(value, axis, step):
    ring = RING[axis]
    return lax.ppermute(value, axis, [(ring[i], ring[(i + step) % 4]) for i in range(4)])


def ahead(value, axis):
    return shifted(value, axis, 1)


def behind(value, axis):
    return shifted(value, axis, 3)


def halves_of(value):
    size = (value.shape[0] + 1) // 2
    return value[:size], value[size:]


def gather_ring(mine, axis):
    before = ahead(mine, axis)
    after = behind(mine, axis)
    far = ahead(halves_of(before)[0], axis), behind(halves_of(after)[1], axis)
    return jnp.stack([mine, after, before]), jnp.concatenate(far, axis=0)


def scatter_ring(parts, axis):
    first, second = halves_of(parts[2])
    first, second = ahead(first, axis), behind(second, axis)
    after, before = halves_of(parts[1]), halves_of(parts[3])
    after = jnp.concatenate([after[0] + first, after[1]], axis=0)
    before = jnp.concatenate([before[0], before[1] + second], axis=0)
    return parts[0] + ahead(after, axis) + behind(before, axis)


def per_device(orbitals, blocks, owner):
    core, y, z = (lax.axis_index(name) for name in ("core", "y", "z"))
    ids = jnp.stack([core, z, (z - y) & 3]).astype(jnp.int32)
    planes = orbitals.shape[1]

    phi = turn(orbitals.reshape(planes, ROWS, WIDTH))
    blocks = blocks.reshape(16, planes, ROWS, WIDTH)
    phi, blocks = lax.optimization_barrier((phi, blocks))
    phi = lax.all_gather(phi, ("y", "x_hi", "x_lo")).reshape(4, 4, planes, ROWS, WIDTH)

    blocks = lax.all_to_all(blocks, ("x_lo", "y", "x_hi"), 0, 0, tiled=True)
    blocks = blocks.reshape(8, 2, planes, ROWS, WIDTH)
    mine = jnp.stack(
        [lax.dynamic_index_in_dim(blocks, owner[r], 0, False) for r in range(ROUNDS)]
    )
    own, own_far = gather_ring(mine, "z")
    other, other_far = other_core(own), other_core(own_far)

    keep, send, local = solve(ids, phi, own, other, own_far, other_far)

    local = lax.psum_scatter(local, ("x_hi", "x_lo"), scatter_dimension=0)
    total = scatter_ring(keep + other_core(send), "z")
    total, local = lax.optimization_barrier((total, local))
    local = local[0] + sum(shifted(local[k], "y", k) for k in (1, 2, 3))
    half = lax.axis_index("x_hi")
    mine = lax.dynamic_index_in_dim(total, half, 1)
    theirs = lax.dynamic_index_in_dim(total, 1 - half, 1)
    theirs = lax.ppermute(theirs, "x_hi", [(0, 1), (1, 0)])
    total = jnp.concatenate(
        [jnp.where(half == 0, mine, theirs), jnp.where(half == 0, theirs, mine)], axis=1
    )
    local = turn(local)
    return (
        local.reshape(1, planes, N * N),
        total.reshape(ROUNDS, 2, planes, N * N),
    )


def solution(mesh):
    fine = Mesh(mesh.devices.reshape(2, 4, 4, 2, 2), ("x_lo", "y", "z", "x_hi", "core"))
    band = ("x_lo", "y")
    grid = ("z", "x_hi", "core")
    return jax.shard_map(
        per_device,
        mesh=fine,
        in_specs=(P(band, grid, None), P(band, grid, None), P()),
        out_specs=(P(band, grid, None), P(None, band, grid, None)),
        check_vma=False,
    )
```
